32 devices in a mesh: seq: 32 (over z, y, x, core).
Axes of the slice: x: 2, y: 2, z: 4, core: 2. Of those that a mesh axis runs over, the one named last changes fastest.
Arguments:
- activations: bfloat16 [65536, 384], P('seq'), may hold values from -6 to 6
- conv_weight: bfloat16 [4, 3, 384, 384], replicated, may hold values from -0.1875 to 0.1875
- conv_bias: float32 [4, 384], replicated, may hold values from -3 to 3
- conv_gain: float32 [4, 384], replicated, may hold values from 0.1 to 1.9
- mlp_gain: float32 [4, 384], replicated, may hold values from 0.1 to 1.9
- w_in: bfloat16 [4, 384, 768], replicated, may hold values from -0.3125 to 0.3125
- w_out: bfloat16 [4, 768, 384], replicated, may hold values from -0.21875 to 0.21875
Outputs:
- channel_major: bfloat16 [384, 65536], P('seq')
The draws below stay inside these ranges and needn't reach their ends.
All inputs are finite; a program needn't handle non-finite values.
Results may differ from the reference program's by a relative error of at most 0.015.
Values may be sent and summed in bfloat16 or wider, within the bound.
No kernel may reach another device: no remote copies, remote signals or barrier semaphores. Data moves between devices by JAX's collectives and lax.ppermute only.
A program may use at most 64 MiB of HBM per device.

```python
import jax
import jax.numpy as jnp
from jax import lax

C = 384
HID = 768
LAYERS = 4
S_DEV = 2048
LENGTH = 65536


def steps_of(own_key, extent, cuts, low, largest):
    level, own = 1.0, jax.random.fold_in(own_key, 6)
    for axis_at, shards_of in cuts:
        heights = jnp.exp(jax.random.uniform(jax.random.fold_in(own, axis_at), (shards_of,), jnp.float32, low / len(cuts), largest / len(cuts)))
        level = level * jnp.repeat(heights, extent[axis_at] // shards_of).reshape([-1 if axis == axis_at else 1 for axis in range(len(extent))])
    return level


def gaussian(key, dims, width, limit, cuts=(), dtype=jnp.bfloat16):
    factor_of = steps_of(key, dims, cuts, -0.22, 0.18) if cuts else 1.0
    entries = jax.random.normal(key, dims, jnp.float32) * width * factor_of
    return jnp.minimum(jnp.maximum(entries, -limit), limit).astype(dtype)


def setup_inputs(seed: int = 0) -> dict:
    key_of = jax.random.split(jax.random.key(seed), 8)
    return {
        "activations": gaussian(key_of[0], (LENGTH, C), 1.0, 6.0, ((0, 32),)),
        "conv_weight": gaussian(key_of[1], (LAYERS, 3, C, C), (3 * C) ** -0.5, 0.1875),
        "conv_bias": gaussian(key_of[2], (LAYERS, C), 0.5, 3.0, (), jnp.float32),
        "conv_gain": jnp.clip(1.0 + 0.18 * jax.random.normal(key_of[3], (LAYERS, C), jnp.float32), 0.1, 1.9),
        "mlp_gain": jnp.clip(1.0 + 0.18 * jax.random.normal(key_of[4], (LAYERS, C), jnp.float32), 0.1, 1.9),
        "w_in": gaussian(key_of[5], (LAYERS, C, HID), C ** -0.5, 0.3125),
        "w_out": gaussian(key_of[6], (LAYERS, HID, C), HID ** -0.5, 0.21875),
    }


def rms_scale(values, gain):
    wide = values.astype(jnp.float32)
    inverse = jax.lax.rsqrt(lax.optimization_barrier(jnp.mean(wide * wide, axis=-1, keepdims=True)) + 1e-06)
    return (wide * inverse * gain[None, :]).astype(jnp.bfloat16)

def reference(activations, conv_weight, conv_bias, conv_gain, mlp_gain, w_in, w_out):
    state = activations
    for layer in range(LAYERS):
        span = S_DEV * 2 ** layer
        normed = rms_scale(state, conv_gain[layer])
        blank = jnp.zeros((span, C), jnp.bfloat16)
        earlier = jnp.concatenate([blank, normed[:-span]], axis=0)
        later = jnp.concatenate([normed[span:], blank], axis=0)
        pre = jnp.dot(earlier, conv_weight[layer, 0], preferred_element_type=jnp.float32)
        pre = pre + jnp.dot(normed, conv_weight[layer, 1], preferred_element_type=jnp.float32)
        pre = pre + jnp.dot(later, conv_weight[layer, 2], preferred_element_type=jnp.float32)
        pre = pre + conv_bias[layer][None, :]
        middle = (state.astype(jnp.float32) + jax.nn.gelu(pre, approximate=False)).astype(jnp.bfloat16)
        inner = rms_scale(middle, mlp_gain[layer])
        hidden = jax.nn.gelu(jnp.dot(inner, w_in[layer], preferred_element_type=jnp.float32), approximate=False).astype(jnp.bfloat16)
        state = (middle.astype(jnp.float32) + jnp.dot(hidden, w_out[layer], preferred_element_type=jnp.float32)).astype(jnp.bfloat16)
    return state.T
```

```python
import functools

import jax
import jax.numpy as jnp
import numpy as np
from jax import lax
from jax.experimental import pallas as pl
from jax.experimental.pallas import tpu as pltpu
from jax.sharding import PartitionSpec as P

AXIS = "seq"
ROWS = 16
VMEM_BYTES = 56 * 2**20


def rms_scale(wide, gain):
    inverse = lax.rsqrt(jnp.mean(wide * wide, axis=-1, keepdims=True) + 1e-06)
    return (wide * inverse * gain).astype(jnp.bfloat16)


def gelu(x):
    return (0.5 * x) * (1.0 + lax.erf(x * np.float32(np.sqrt(0.5))))


def dot(a, b):
    return jnp.dot(a, b, preferred_element_type=jnp.float32)


def tower_kernel(
    tile, unit, groups, x_ref, taps_ref, bias_ref, gain_conv_ref, gain_mlp_ref, in_ref, out_ref, pick_ref,
    y_ref, state_ref, normed_ref,
):
    layer = pl.program_id(0)
    layers = pl.num_programs(0)
    rows, channels = x_ref.shape
    pad = (normed_ref.shape[1] - rows) // 2
    now = lax.rem(layer, 2)

    @pl.when(layer == 0)
    def _():
        for slot in range(2):
            normed_ref[slot, :pad] = jnp.zeros((pad, channels), jnp.bfloat16)
            normed_ref[slot, pad + rows :] = jnp.zeros((pad, channels), jnp.bfloat16)
        for start in range(0, rows, tile):
            block = x_ref[start : start + tile]
            state_ref[start : start + tile] = block
            normed_ref[0, pad + start : pad + start + tile] = rms_scale(block.astype(jnp.float32), gain_conv_ref[0:1])

    shift = lax.shift_left(unit, layer)
    gain_next = gain_conv_ref[pl.ds(jnp.minimum(layer + 1, layers - 1), 1)]

    def step(i, carry):
        start = pl.multiple_of(i * tile, tile)
        base = pad + start
        near = [
            normed_ref[now, pl.ds(pl.multiple_of(base + offset, ROWS), tile)] for offset in (-shift, 0, shift)
        ]
        pre = dot(jnp.concatenate(near, axis=1), taps_ref[0]) + bias_ref[pl.ds(layer, 1)]
        wide = state_ref[pl.ds(start, tile)].astype(jnp.float32)
        middle = (wide + gelu(pre)).astype(jnp.bfloat16).astype(jnp.float32)
        inner = rms_scale(middle, gain_mlp_ref[pl.ds(layer, 1)])
        hidden = gelu(dot(inner, in_ref[0])).astype(jnp.bfloat16)
        new = (middle + dot(hidden, out_ref[0])).astype(jnp.bfloat16)
        state_ref[pl.ds(start, tile)] = new
        normed_ref[1 - now, pl.ds(pl.multiple_of(base, ROWS), tile)] = rms_scale(new.astype(jnp.float32), gain_next)
        return carry

    lax.fori_loop(0, rows // tile, step, 0)

    @pl.when(layer == layers - 1)
    def _():
        width = y_ref.shape[1] // groups
        for g in range(groups):
            part = state_ref[g * width : (g + 1) * width]
            if groups > 1:
                part = jnp.concatenate([part, state_ref[groups * width :]], axis=1)
            y_ref[:, g * width : (g + 1) * width] = lax.dot_general(
                pick_ref[g], part, (((1,), (1,)), ((), ())), preferred_element_type=jnp.float32
            ).astype(jnp.bfloat16)


def picker(channels, per, groups):
    if groups == 1:
        return np.eye(channels, dtype=np.float32)[None].astype(jnp.bfloat16)
    extra = per // groups
    pick = np.zeros((groups, channels // per * ROWS, 2 * channels), np.float32)
    for g in range(groups):
        for owner in range(channels // per):
            for r in range(per):
                pick[g, owner * ROWS + r, owner * per + r] = 1
            for r in range(extra):
                pick[g, owner * ROWS + per + r, channels + owner * per + g * extra + r] = 1
    return pick.astype(jnp.bfloat16)


def tower(x, conv_weight, conv_bias, conv_gain, mlp_gain, w_in, w_out, unit, per, groups):
    rows, channels = x.shape
    layers, _, hidden = w_in.shape
    pick = picker(channels, per, groups)
    out_shape = (pick.shape[1], rows // (groups + 1) * groups if groups > 1 else rows)
    pad = unit * 2 ** (layers - 1)
    tile = rows

    def whole(shape):
        return pl.BlockSpec(shape, lambda layer: (0,) * len(shape))

    def of_layer(*shape):
        return pl.BlockSpec((1, *shape), lambda layer: (layer, 0, 0))

    return pl.pallas_call(
        functools.partial(tower_kernel, tile, unit, groups),
        grid=(layers,),
        in_specs=[
            whole(x.shape),
            of_layer(3 * channels, channels),
            whole(conv_bias.shape),
            whole(conv_gain.shape),
            whole(mlp_gain.shape),
            of_layer(channels, hidden),
            of_layer(hidden, channels),
            whole(pick.shape),
        ],
        out_specs=whole(out_shape),
        out_shape=jax.ShapeDtypeStruct(out_shape, jnp.bfloat16),
        scratch_shapes=[
            pltpu.VMEM((rows, channels), jnp.bfloat16),
            pltpu.VMEM((2, rows + 2 * pad, channels), jnp.bfloat16),
        ],
        compiler_params=pltpu.CompilerParams(vmem_limit_bytes=VMEM_BYTES),
        name="tower",
    )(
        x,
        conv_weight.reshape(layers, 3 * channels, channels),
        conv_bias,
        conv_gain,
        mlp_gain,
        w_in,
        w_out,
        jnp.asarray(pick),
    )


def weave_kernel(per, groups, unit, x_ref, y_ref):
    sources, _, width = x_ref.shape
    extra, part = per // groups, width // groups
    block_rows = unit * sources

    def unpacked(source):
        rows = x_ref[source].astype(jnp.float32)
        rest = [rows[per : per + extra, g * part : (g + 1) * part] for g in range(groups)]
        return jnp.concatenate([rows[:per], jnp.concatenate(rest, axis=0)], axis=1)

    def step(pair, carry):
        even, odd = unpacked(2 * pair), unpacked(2 * pair + 1)
        low = lax.broadcasted_iota(jnp.int32, (per, 2 * unit), 1) < unit
        for m in range(sources // 2):
            cut = slice(2 * unit * m, 2 * unit * (m + 1))
            a, b = even[:, cut], odd[:, cut]
            for block, value in (
                (2 * m, jnp.where(low, a, pltpu.roll(b, unit, 1))),
                (2 * m + 1, jnp.where(low, pltpu.roll(a, unit, 1), b)),
            ):
                at = pl.multiple_of(block * block_rows + pair * 2 * unit, 2 * unit)
                y_ref[:, pl.ds(at, 2 * unit)] = value.astype(jnp.bfloat16)
        return carry

    lax.fori_loop(0, sources // 2, step, 0)


def weave(x, per, groups, unit, rows):
    sources = x.shape[0]
    return pl.pallas_call(
        functools.partial(weave_kernel, per, groups, unit),
        out_shape=jax.ShapeDtypeStruct((per, sources * rows), jnp.bfloat16),
        compiler_params=pltpu.CompilerParams(vmem_limit_bytes=VMEM_BYTES),
        name="weave",
    )(x)


def shards(activations, conv_weight, conv_bias, conv_gain, mlp_gain, w_in, w_out):
    devices = lax.axis_size(AXIS)
    rows, channels = activations.shape
    unit, per = rows // devices, channels // devices
    x = lax.all_to_all(activations, AXIS, split_axis=0, concat_axis=0, tiled=True)
    spare = ROWS - per
    groups = per // spare if 0 < spare < per and per % spare == 0 else 1
    fits = groups > 1 and 2 * unit == 128 and rows % ((groups + 1) * 128) == 0
    if not fits:
        groups = 1
    y = tower(x, conv_weight, conv_bias, conv_gain, mlp_gain, w_in, w_out, unit, per, groups)
    if fits:
        y = lax.all_to_all(y.reshape(devices, ROWS, -1), AXIS, split_axis=0, concat_axis=0, tiled=True)
        return weave(y, per, groups, unit, rows)
    y = lax.all_to_all(y.reshape(devices, per, rows), AXIS, split_axis=0, concat_axis=0, tiled=True)
    y = y.reshape(devices, per, devices, unit).transpose(1, 2, 0, 3)
    return y.reshape(per, devices * rows)


def solution(mesh):
    in_specs = (P(AXIS, None), P(), P(), P(), P(), P(), P())
    return jax.shard_map(shards, mesh=mesh, in_specs=in_specs, out_specs=P(AXIS, None), check_vma=False)
```

```python
import functools

import jax
import jax.numpy as jnp
import numpy as np
from jax import lax
from jax.experimental import pallas as pl
from jax.experimental.pallas import tpu as pltpu
from jax.sharding import PartitionSpec as P

AXIS = "seq"
CHUNKS = 2
ROWS = 16
VMEM_BYTES = 56 * 2**20


def rms_scale(wide, gain):
    inverse = lax.rsqrt(jnp.mean(wide * wide, axis=-1, keepdims=True) + 1e-06)
    return (wide * inverse * gain).astype(jnp.bfloat16)


def gelu(x):
    return (0.5 * x) * (1.0 + lax.erf(x * np.float32(np.sqrt(0.5))))


def dot(a, b):
    return jnp.dot(a, b, preferred_element_type=jnp.float32)


def tower_kernel(
    tile, unit, groups, x_ref, taps_ref, bias_ref, gain_conv_ref, gain_mlp_ref, in_ref, out_ref, pick_ref,
    y_ref, state_ref, normed_ref,
):
    layer = pl.program_id(0)
    layers = pl.num_programs(0)
    rows, channels = x_ref.shape
    pad = (normed_ref.shape[1] - rows) // 2
    now = lax.rem(layer, 2)

    @pl.when(layer == 0)
    def _():
        for slot in range(2):
            normed_ref[slot, :pad] = jnp.zeros((pad, channels), jnp.bfloat16)
            normed_ref[slot, pad + rows :] = jnp.zeros((pad, channels), jnp.bfloat16)
        for start in range(0, rows, tile):
            block = x_ref[start : start + tile]
            state_ref[start : start + tile] = block
            normed_ref[0, pad + start : pad + start + tile] = rms_scale(block.astype(jnp.float32), gain_conv_ref[0:1])

    shift = lax.shift_left(unit, layer)
    gain_next = gain_conv_ref[pl.ds(jnp.minimum(layer + 1, layers - 1), 1)]

    def step(i, carry):
        start = pl.multiple_of(i * tile, tile)
        base = pad + start
        near = [
            normed_ref[now, pl.ds(pl.multiple_of(base + offset, ROWS), tile)] for offset in (-shift, 0, shift)
        ]
        pre = dot(jnp.concatenate(near, axis=1), taps_ref[0]) + bias_ref[pl.ds(layer, 1)]
        wide = state_ref[pl.ds(start, tile)].astype(jnp.float32)
        middle = (wide + gelu(pre)).astype(jnp.bfloat16).astype(jnp.float32)
        inner = rms_scale(middle, gain_mlp_ref[pl.ds(layer, 1)])
        hidden = gelu(dot(inner, in_ref[0])).astype(jnp.bfloat16)
        new = (middle + dot(hidden, out_ref[0])).astype(jnp.bfloat16)
        state_ref[pl.ds(start, tile)] = new
        normed_ref[1 - now, pl.ds(pl.multiple_of(base, ROWS), tile)] = rms_scale(new.astype(jnp.float32), gain_next)
        return carry

    lax.fori_loop(0, rows // tile, step, 0)

    @pl.when(layer == layers - 1)
    def _():
        width = y_ref.shape[1] // groups
        for g in range(groups):
            part = state_ref[g * width : (g + 1) * width]
            if groups > 1:
                part = jnp.concatenate([part, state_ref[groups * width :]], axis=1)
            y_ref[:, g * width : (g + 1) * width] = lax.dot_general(
                pick_ref[g], part, (((1,), (1,)), ((), ())), preferred_element_type=jnp.float32
            ).astype(jnp.bfloat16)


def picker(channels, per, groups):
    if groups == 1:
        return np.eye(channels, dtype=np.float32)[None].astype(jnp.bfloat16)
    extra = per // groups
    pick = np.zeros((groups, channels // per * ROWS, 2 * channels), np.float32)
    for g in range(groups):
        for owner in range(channels // per):
            for r in range(per):
                pick[g, owner * ROWS + r, owner * per + r] = 1
            for r in range(extra):
                pick[g, owner * ROWS + per + r, channels + owner * per + g * extra + r] = 1
    return pick.astype(jnp.bfloat16)


def tower(x, conv_weight, conv_bias, conv_gain, mlp_gain, w_in, w_out, unit, per, groups):
    rows, channels = x.shape
    layers, _, hidden = w_in.shape
    pick = picker(channels, per, groups)
    out_shape = (pick.shape[1], rows // (groups + 1) * groups if groups > 1 else rows)
    pad = unit * 2 ** (layers - 1)
    tile = rows

    def whole(shape):
        return pl.BlockSpec(shape, lambda layer: (0,) * len(shape))

    def of_layer(*shape):
        return pl.BlockSpec((1, *shape), lambda layer: (layer, 0, 0))

    return pl.pallas_call(
        functools.partial(tower_kernel, tile, unit, groups),
        grid=(layers,),
        in_specs=[
            whole(x.shape),
            of_layer(3 * channels, channels),
            whole(conv_bias.shape),
            whole(conv_gain.shape),
            whole(mlp_gain.shape),
            of_layer(channels, hidden),
            of_layer(hidden, channels),
            whole(pick.shape),
        ],
        out_specs=whole(out_shape),
        out_shape=jax.ShapeDtypeStruct(out_shape, jnp.bfloat16),
        scratch_shapes=[
            pltpu.VMEM((rows, channels), jnp.bfloat16),
            pltpu.VMEM((2, rows + 2 * pad, channels), jnp.bfloat16),
        ],
        cost_estimate=pl.CostEstimate(
            flops=2 * rows * conv_weight.size + 4 * rows * w_in.size,
            bytes_accessed=2 * (conv_weight.size + 2 * w_in.size + 2 * x.size),
            transcendentals=layers * rows * (channels + hidden),
        ),
        compiler_params=pltpu.CompilerParams(vmem_limit_bytes=VMEM_BYTES),
        name="tower",
    )(
        x,
        conv_weight.reshape(layers, 3 * channels, channels),
        conv_bias,
        conv_gain,
        mlp_gain,
        w_in,
        w_out,
        jnp.asarray(pick),
    )


def weaver(units):
    lanes = 128 // units
    weave_of = np.zeros((lanes, lanes, units, lanes, lanes, units), np.float32)
    for source in range(lanes):
        for block in range(lanes):
            weave_of[source, block, range(units), block, source, range(units)] = 1
    return weave_of.reshape(lanes * 128, lanes * 128).astype(jnp.bfloat16)


def weave_kernel(per, groups, unit, first, stride, x_ref, weave_ref, *refs):
    y_ref, woven_ref, sems = refs[-3:]
    sources, _, width = x_ref.shape
    extra, part = per // groups, width // groups
    span = unit * sources
    lanes = 128 // unit
    tiles = width // 128
    part_tiles = part // 128
    whole_blocks = tiles * lanes
    for top in range(sources // lanes):
        rows = [
            jnp.concatenate(
                [x_ref[top * lanes + source, :, t * 128 : (t + 1) * 128] for source in range(lanes)], axis=1
            )
            for t in range(tiles)
        ]
        swapped = dot(jnp.concatenate(rows, axis=0), weave_ref[...])

        def piece(t, b, low, high):
            return swapped[t * ROWS + low : t * ROWS + high, b * 128 : (b + 1) * 128]

        for b in range(lanes):
            for t in range(tiles):
                at = (t * lanes + b) * span + top * 128
                woven_ref[:, at : at + 128] = piece(t, b, 0, per).astype(jnp.bfloat16)
            for t in range(part_tiles):
                at = (whole_blocks + t * lanes + b) * span + top * 128
                rest = [piece(g * part_tiles + t, b, per, per + extra) for g in range(groups)]
                woven_ref[:, at : at + 128] = jnp.concatenate(rest, axis=0).astype(jnp.bfloat16)
    copies = [
        pltpu.make_async_copy(
            woven_ref.at[:, pl.ds(block * span, span)],
            y_ref.at[:, pl.ds(block * stride + first, span)],
            sems.at[block],
        )
        for block in range(sources)
    ]
    for copy in copies:
        copy.start()
    for copy in copies:
        copy.wait()


def weave(x, y, per, groups, unit, first, stride):
    sources = x.shape[0]
    vmem = pl.BlockSpec(memory_space=pltpu.VMEM)
    operands = [x, jnp.asarray(weaver(unit))] + ([] if y is None else [y])
    return pl.pallas_call(
        functools.partial(weave_kernel, per, groups, unit, first, stride),
        in_specs=[vmem, vmem] + ([] if y is None else [pl.BlockSpec(memory_space=pl.ANY)]),
        out_specs=pl.BlockSpec(memory_space=pl.ANY),
        out_shape=jax.ShapeDtypeStruct((per, sources * stride), jnp.bfloat16),
        scratch_shapes=[
            pltpu.VMEM((per, sources * unit * sources), jnp.bfloat16),
            pltpu.SemaphoreType.DMA((sources,)),
        ],
        input_output_aliases={} if y is None else {2: 0},
        compiler_params=pltpu.CompilerParams(vmem_limit_bytes=VMEM_BYTES),
        name="weave",
    )(*operands)


def exchange(x):
    return lax.all_to_all(x, AXIS, split_axis=0, concat_axis=0, tiled=True)


def shards(activations, conv_weight, conv_bias, conv_gain, mlp_gain, w_in, w_out):
    devices = lax.axis_size(AXIS)
    rows, channels = activations.shape
    unit, per = rows // devices, channels // devices
    weights = (conv_weight, conv_bias, conv_gain, mlp_gain, w_in, w_out)
    spare = ROWS - per
    groups = per // spare if 0 < spare < per and per % spare == 0 else 1
    part = unit // CHUNKS
    if groups > 1 and part % ROWS == 0 and part * devices % ((groups + 1) * 128) == 0 and devices * part % 128 == 0:
        size = rows // CHUNKS
        y = None
        towers = []
        for c in range(CHUNKS):
            x = exchange(activations[c * size : (c + 1) * size])
            towers.append(tower(x, *weights, part, per, groups))
        for c in range(CHUNKS):
            x = exchange(towers[c].reshape(devices, ROWS, -1))
            y = weave(x, y, per, groups, part, c * size, rows)
        return y
    y = tower(exchange(activations), *weights, unit, per, 1)
    y = exchange(y.reshape(devices, per, rows))
    y = y.reshape(devices, per, devices, unit).transpose(1, 2, 0, 3)
    return y.reshape(per, devices * rows)


def solution(mesh):
    in_specs = (P(AXIS, None), P(), P(), P(), P(), P(), P())
    return jax.shard_map(shards, mesh=mesh, in_specs=in_specs, out_specs=P(AXIS, None), check_vma=False)
```

```python
import functools

import jax
import jax.numpy as jnp
import numpy as np
from jax import lax
from jax.experimental import pallas as pl
from jax.experimental.pallas import tpu as pltpu
from jax.sharding import PartitionSpec as P

AXIS = "seq"
CHUNKS = 2
TILE = 256
ROWS = 16


def rms_scale(wide, gain):
    inverse = lax.rsqrt(jnp.mean(wide * wide, axis=-1, keepdims=True) + 1e-06)
    return (wide * inverse * gain).astype(jnp.bfloat16)


def gelu(x):
    return (0.5 * x) * (1.0 + lax.erf(x * np.float32(np.sqrt(0.5))))


def dot(a, b):
    return jnp.dot(a, b, preferred_element_type=jnp.float32)


def tower_kernel(
    tile, unit, groups, x_ref, taps_ref, bias_ref, gain_conv_ref, gain_mlp_ref, in_ref, out_ref, pick_ref,
    y_ref, state_ref, normed_ref,
):
    layer = pl.program_id(0)
    layers = pl.num_programs(0)
    rows, channels = x_ref.shape
    pad = (normed_ref.shape[1] - rows) // 2
    now = lax.rem(layer, 2)

    @pl.when(layer == 0)
    def _():
        for slot in range(2):
            normed_ref[slot, :pad] = jnp.zeros((pad, channels), jnp.bfloat16)
            normed_ref[slot, pad + rows :] = jnp.zeros((pad, channels), jnp.bfloat16)
        for start in range(0, rows, tile):
            block = x_ref[start : start + tile]
            state_ref[start : start + tile] = block
            normed_ref[0, pad + start : pad + start + tile] = rms_scale(block.astype(jnp.float32), gain_conv_ref[0:1])

    shift = lax.shift_left(unit, layer)
    gain_next = gain_conv_ref[pl.ds(jnp.minimum(layer + 1, layers - 1), 1)]

    bias, gain_mlp = bias_ref[pl.ds(layer, 1)], gain_mlp_ref[pl.ds(layer, 1)]
    starts = range(0, rows, tile)

    def mixed(start):
        near = [
            normed_ref[now, pl.ds(pl.multiple_of(pad + start + offset, ROWS), tile)] for offset in (-shift, 0, shift)
        ]
        pre = dot(jnp.concatenate(near, axis=1), taps_ref[0]) + bias
        return (state_ref[start : start + tile].astype(jnp.float32) + gelu(pre)).astype(jnp.bfloat16)

    def widened(middle):
        inner = rms_scale(middle.astype(jnp.float32), gain_mlp)
        return gelu(dot(inner, in_ref[0])).astype(jnp.bfloat16)

    middles = [mixed(start) for start in starts]
    hiddens = [widened(middle) for middle in middles]
    for start, middle, hidden in zip(starts, middles, hiddens):
        new = (middle.astype(jnp.float32) + dot(hidden, out_ref[0])).astype(jnp.bfloat16)
        state_ref[start : start + tile] = new
        normed_ref[1 - now, pad + start : pad + start + tile] = rms_scale(new.astype(jnp.float32), gain_next)

    @pl.when(layer == layers - 1)
    def _():
        width = y_ref.shape[1] // groups
        for g in range(groups):
            part = state_ref[g * width : (g + 1) * width]
            if groups > 1:
                part = jnp.concatenate([part, state_ref[groups * width :]], axis=1)
            y_ref[:, g * width : (g + 1) * width] = lax.dot_general(
                pick_ref[g], part, (((1,), (1,)), ((), ())), preferred_element_type=jnp.float32
            ).astype(jnp.bfloat16)


def picker(channels, per, groups):
    if groups == 1:
        return np.eye(channels, dtype=np.float32)[None].astype(jnp.bfloat16)
    extra = per // groups
    pick = np.zeros((groups, channels // per * ROWS, 2 * channels), np.float32)
    for g in range(groups):
        for owner in range(channels // per):
            for r in range(per):
                pick[g, owner * ROWS + r, owner * per + r] = 1
            for r in range(extra):
                pick[g, owner * ROWS + per + r, channels + owner * per + g * extra + r] = 1
    return pick.astype(jnp.bfloat16)


def tower(x, conv_weight, conv_bias, conv_gain, mlp_gain, w_in, w_out, unit, per, groups):
    rows, channels = x.shape
    layers, _, hidden = w_in.shape
    pick = picker(channels, per, groups)
    out_shape = (pick.shape[1], rows // (groups + 1) * groups if groups > 1 else rows)
    pad = unit * 2 ** (layers - 1)
    tile = TILE if rows % TILE == 0 else rows

    def whole(shape):
        return pl.BlockSpec(shape, lambda layer: (0,) * len(shape))

    def of_layer(*shape):
        return pl.BlockSpec((1, *shape), lambda layer: (layer, 0, 0))

    return pl.pallas_call(
        functools.partial(tower_kernel, tile, unit, groups),
        grid=(layers,),
        in_specs=[
            whole(x.shape),
            of_layer(3 * channels, channels),
            whole(conv_bias.shape),
            whole(conv_gain.shape),
            whole(mlp_gain.shape),
            of_layer(channels, hidden),
            of_layer(hidden, channels),
            whole(pick.shape),
        ],
        out_specs=whole(out_shape),
        out_shape=jax.ShapeDtypeStruct(out_shape, jnp.bfloat16),
        scratch_shapes=[
            pltpu.VMEM((rows, channels), jnp.bfloat16),
            pltpu.VMEM((2, rows + 2 * pad, channels), jnp.bfloat16),
        ],
        cost_estimate=pl.CostEstimate(
            flops=2 * rows * conv_weight.size + 4 * rows * w_in.size,
            bytes_accessed=2 * (conv_weight.size + 2 * w_in.size + 2 * x.size),
            transcendentals=layers * rows * (channels + hidden),
        ),
        compiler_params=pltpu.CompilerParams(vmem_limit_bytes=56 * 2**20),
        name="tower",
    )(
        x,
        conv_weight.reshape(layers, 3 * channels, channels),
        conv_bias,
        conv_gain,
        mlp_gain,
        w_in,
        w_out,
        jnp.asarray(pick),
    )


def weaver(units):
    lanes = 128 // units
    weave_of = np.zeros((lanes, lanes, units, lanes, lanes, units), np.float32)
    for source in range(lanes):
        for block in range(lanes):
            weave_of[source, block, range(units), block, source, range(units)] = 1
    return weave_of.reshape(lanes * 128, lanes * 128).astype(jnp.bfloat16)


def weave_kernel(per, groups, unit, first, stride, x_ref, weave_ref, *refs):
    y_ref, woven_ref, sems = refs[-3:]
    sources, _, width = x_ref.shape
    extra, part = per // groups, width // groups
    span = unit * sources
    lanes = 128 // unit
    tops, tiles, part_tiles = sources // lanes, width // 128, part // 128
    copies = [
        pltpu.make_async_copy(
            woven_ref.at[:, pl.ds(block * span, span)],
            y_ref.at[:, pl.ds(block * stride + first, span)],
            sems.at[block],
        )
        for block in range(sources)
    ]

    def put(block, top, value):
        at = block * span + top * 128
        woven_ref[:, at : at + 128] = value.astype(jnp.bfloat16)

    swapped = []
    for t in range(tiles):
        cut = slice(t * 128, (t + 1) * 128)
        rows = [
            jnp.concatenate([x_ref[top * lanes + source, :, cut] for source in range(lanes)], axis=1)
            for top in range(tops)
        ]
        swapped.append(dot(jnp.concatenate(rows, axis=0), weave_ref[...]))
        for b in range(lanes):
            for top in range(tops):
                low = top * ROWS
                put(t * lanes + b, top, swapped[t][low : low + per, b * 128 : (b + 1) * 128])
            copies[t * lanes + b].start()
    for t in range(part_tiles):
        for b in range(lanes):
            block = (tiles + t) * lanes + b
            for top in range(tops):
                low = top * ROWS + per
                rest = [
                    swapped[g * part_tiles + t][low : low + extra, b * 128 : (b + 1) * 128] for g in range(groups)
                ]
                put(block, top, jnp.concatenate(rest, axis=0))
            copies[block].start()
    for copy in copies:
        copy.wait()


def weave(x, y, per, groups, unit, first, stride):
    sources = x.shape[0]
    vmem, anywhere = pl.BlockSpec(memory_space=pltpu.VMEM), pl.BlockSpec(memory_space=pl.ANY)
    operands = [x, jnp.asarray(weaver(unit))] + ([] if y is None else [y])
    return pl.pallas_call(
        functools.partial(weave_kernel, per, groups, unit, first, stride),
        in_specs=[vmem, vmem] + ([] if y is None else [anywhere]),
        out_specs=anywhere,
        out_shape=jax.ShapeDtypeStruct((per, sources * stride), jnp.bfloat16),
        scratch_shapes=[
            pltpu.VMEM((per, sources * unit * sources), jnp.bfloat16),
            pltpu.SemaphoreType.DMA((sources,)),
        ],
        input_output_aliases={} if y is None else {2: 0},
        compiler_params=pltpu.CompilerParams(vmem_limit_bytes=12 * 2**20),
        name="weave",
    )(*operands)


def exchange(x):
    return lax.all_to_all(x, AXIS, split_axis=0, concat_axis=0, tiled=True)


def shards(activations, conv_weight, conv_bias, conv_gain, mlp_gain, w_in, w_out):
    devices = lax.axis_size(AXIS)
    rows, channels = activations.shape
    unit, per = rows // devices, channels // devices
    weights = (conv_weight, conv_bias, conv_gain, mlp_gain, w_in, w_out)
    spare = ROWS - per
    groups = per // spare if 0 < spare < per and per % spare == 0 else 1
    part = unit // CHUNKS
    if groups > 1 and part % ROWS == 0 and part * devices % ((groups + 1) * 128) == 0 and devices * part % 128 == 0:
        size = rows // CHUNKS
        y = None
        towers = []
        for c in range(CHUNKS):
            whole = activations if c == 0 else lax.optimization_barrier(activations)
            x = exchange(whole[c * size : (c + 1) * size])
            towers.append(tower(x, *weights, part, per, groups))
        for c in range(CHUNKS):
            x = exchange(towers[c].reshape(devices, ROWS, -1))
            y = weave(x, y, per, groups, part, c * size, rows)
        return y
    y = tower(exchange(activations), *weights, unit, per, 1)
    y = exchange(y.reshape(devices, per, rows))
    y = y.reshape(devices, per, devices, unit).transpose(1, 2, 0, 3)
    return y.reshape(per, devices * rows)


def solution(mesh):
    in_specs = (P(AXIS, None), P(), P(), P(), P(), P(), P())
    return jax.shard_map(shards, mesh=mesh, in_specs=in_specs, out_specs=P(AXIS, None), check_vma=False)
```

```python
import functools

import jax
import jax.numpy as jnp
import numpy as np
from jax import lax
from jax.experimental import pallas as pl
from jax.experimental.pallas import tpu as pltpu
from jax.sharding import PartitionSpec as P

AXIS = "seq"
CHUNKS = 2
TIE = 1
STAGES = ((3, 2), (1, 2), (0, 1))
TILE = 256
ROWS = 16


def rms_scale(wide, gain):
    inverse = lax.rsqrt(jnp.mean(wide * wide, axis=-1, keepdims=True) + 1e-06)
    return (wide * inverse * gain).astype(jnp.bfloat16)


def gelu(x):
    return (0.5 * x) * (1.0 + lax.erf(x * np.float32(np.sqrt(0.5))))


def dot(a, b):
    return jnp.dot(a, b, preferred_element_type=jnp.float32)


def tower_kernel(
    tile, unit, groups, layout, me_ref, taps_ref, bias_ref, gain_conv_ref, gain_mlp_ref, in_ref, out_ref, pick_hbm, *refs
):
    *x_refs, y_ref, pick_ref, state_ref, normed_ref, sem = refs
    fetch = pltpu.make_async_copy(pick_hbm, pick_ref, sem)
    layer = pl.program_id(0)
    layers = pl.num_programs(0)
    rows, channels = state_ref.shape
    pad = (normed_ref.shape[1] - rows) // 2
    now = lax.rem(layer, 2)

    @pl.when(layer == 0)
    def _():
        for slot in range(2):
            normed_ref[slot, :pad] = jnp.zeros((pad, channels), jnp.bfloat16)
            normed_ref[slot, pad + rows :] = jnp.zeros((pad, channels), jnp.bfloat16)
        for x_ref, (blocks, relative, offset) in zip(x_refs, layout):
            width = x_ref.shape[0] // len(blocks)
            if width == unit and not relative:
                state_ref[...] = x_ref[...]
                continue
            for i, block in enumerate(blocks):
                block = lax.bitwise_xor(me_ref[0], block) if relative else block
                at = pl.multiple_of(block * unit + offset, ROWS)
                state_ref[pl.ds(at, width)] = x_ref[i * width : (i + 1) * width]
        for start in range(0, rows, tile):
            wide = state_ref[start : start + tile].astype(jnp.float32)
            normed_ref[0, pad + start : pad + start + tile] = rms_scale(wide, gain_conv_ref[0:1])

    @pl.when(layer == layers - 2)
    def _():
        fetch.start()

    shift = lax.shift_left(unit, layer)
    gain_next = gain_conv_ref[pl.ds(jnp.minimum(layer + 1, layers - 1), 1)]

    bias, gain_mlp = bias_ref[pl.ds(layer, 1)], gain_mlp_ref[pl.ds(layer, 1)]
    starts = range(0, rows, tile)

    def mixed(start):
        near = [
            normed_ref[now, pl.ds(pl.multiple_of(pad + start + offset, ROWS), tile)] for offset in (-shift, 0, shift)
        ]
        pre = dot(jnp.concatenate(near, axis=1), taps_ref[0]) + bias
        return (state_ref[start : start + tile].astype(jnp.float32) + gelu(pre)).astype(jnp.bfloat16)

    def widened(middle):
        inner = rms_scale(middle.astype(jnp.float32), gain_mlp)
        return gelu(dot(inner, in_ref[0])).astype(jnp.bfloat16)

    middles = [mixed(start) for start in starts]
    hiddens = [widened(middle) for middle in middles]
    for start, middle, hidden in zip(starts, middles, hiddens):
        new = (middle.astype(jnp.float32) + dot(hidden, out_ref[0])).astype(jnp.bfloat16)
        state_ref[start : start + tile] = new
        normed_ref[1 - now, pad + start : pad + start + tile] = rms_scale(new.astype(jnp.float32), gain_next)

    @pl.when(layer == layers - 1)
    def _():
        fetch.wait()
        width = y_ref.shape[1] // groups
        for g in range(groups):
            part = state_ref[g * width : (g + 1) * width]
            if groups > 1:
                part = jnp.concatenate([part, state_ref[groups * width :]], axis=1)
            y_ref[:, g * width : (g + 1) * width] = lax.dot_general(
                pick_ref[g], part, (((1,), (1,)), ((), ())), preferred_element_type=jnp.float32
            ).astype(jnp.bfloat16)


def picker(channels, per, groups):
    if groups == 1:
        return np.eye(channels, dtype=np.float32)[None].astype(jnp.bfloat16)
    extra = per // groups
    pick = np.zeros((groups, channels // per * ROWS, 2 * channels), np.float32)
    for g in range(groups):
        for owner in range(channels // per):
            for r in range(per):
                pick[g, owner * ROWS + r, owner * per + r] = 1
            for r in range(extra):
                pick[g, owner * ROWS + per + r, channels + owner * per + g * extra + r] = 1
    return pick.astype(jnp.bfloat16)


def tower(parts, layout, conv_weight, conv_bias, conv_gain, mlp_gain, w_in, w_out, unit, per, groups):
    rows, channels = sum(part.shape[0] for part in parts), parts[0].shape[1]
    layers, _, hidden = w_in.shape
    pick = picker(channels, per, groups)
    out_shape = (pick.shape[1], rows // (groups + 1) * groups if groups > 1 else rows)
    pad = unit * 2 ** (layers - 1)
    tile = TILE if rows % TILE == 0 else rows

    anywhere = pl.BlockSpec(memory_space=pl.ANY)

    def whole(shape):
        return pl.BlockSpec(shape, lambda layer: (0,) * len(shape))

    def of_layer(*shape):
        return pl.BlockSpec((1, *shape), lambda layer: (layer, 0, 0))

    return pl.pallas_call(
        functools.partial(tower_kernel, tile, unit, groups, layout),
        grid=(layers,),
        in_specs=[
            pl.BlockSpec(memory_space=pltpu.SMEM),
            of_layer(3 * channels, channels),
            whole(conv_bias.shape),
            whole(conv_gain.shape),
            whole(mlp_gain.shape),
            of_layer(channels, hidden),
            of_layer(hidden, channels),
            anywhere,
            *[whole(part.shape) for part in parts],
        ],
        out_specs=whole(out_shape),
        out_shape=jax.ShapeDtypeStruct(out_shape, jnp.bfloat16),
        scratch_shapes=[
            pltpu.VMEM(pick.shape, jnp.bfloat16),
            pltpu.VMEM((rows, channels), jnp.bfloat16),
            pltpu.VMEM((2, rows + 2 * pad, channels), jnp.bfloat16),
            pltpu.SemaphoreType.DMA,
        ],
        cost_estimate=pl.CostEstimate(
            flops=2 * rows * conv_weight.size + 4 * rows * w_in.size,
            bytes_accessed=2 * (conv_weight.size + 2 * w_in.size + 2 * rows * channels),
            transcendentals=layers * rows * (channels + hidden),
        ),
        compiler_params=pltpu.CompilerParams(vmem_limit_bytes=56 * 2**20),
        name="tower",
    )(
        lax.axis_index(AXIS).reshape(1).astype(jnp.int32),
        conv_weight.reshape(layers, 3 * channels, channels),
        conv_bias,
        conv_gain,
        mlp_gain,
        w_in,
        w_out,
        jnp.asarray(pick),
        *parts,
    )


def weaver(units):
    lanes = 128 // units
    weave_of = np.zeros((lanes, lanes, units, lanes, lanes, units), np.float32)
    for source in range(lanes):
        for block in range(lanes):
            weave_of[source, block, range(units), block, source, range(units)] = 1
    return weave_of.reshape(lanes * 128, lanes * 128).astype(jnp.bfloat16)


def weave_kernel(per, groups, unit, first, stride, x_ref, weave_ref, *refs):
    y_ref, woven_ref, sems = refs[-3:]
    sources, _, width = x_ref.shape
    extra, part = per // groups, width // groups
    span = unit * sources
    lanes = 128 // unit
    tops, tiles, part_tiles = sources // lanes, width // 128, part // 128
    copies = [
        pltpu.make_async_copy(
            woven_ref.at[:, pl.ds(block * span, span)],
            y_ref.at[:, pl.ds(block * stride + first, span)],
            sems.at[block],
        )
        for block in range(sources)
    ]

    def put(block, top, value):
        at = block * span + top * 128
        woven_ref[:, at : at + 128] = value.astype(jnp.bfloat16)

    swapped = []
    for t in range(tiles):
        cut = slice(t * 128, (t + 1) * 128)
        rows = [
            jnp.concatenate([x_ref[top * lanes + source, :, cut] for source in range(lanes)], axis=1)
            for top in range(tops)
        ]
        swapped.append(dot(jnp.concatenate(rows, axis=0), weave_ref[...]))
        for b in range(lanes):
            for top in range(tops):
                low = top * ROWS
                put(t * lanes + b, top, swapped[t][low : low + per, b * 128 : (b + 1) * 128])
            copies[t * lanes + b].start()
    for t in range(part_tiles):
        for b in range(lanes):
            block = (tiles + t) * lanes + b
            for top in range(tops):
                low = top * ROWS + per
                rest = [
                    swapped[g * part_tiles + t][low : low + extra, b * 128 : (b + 1) * 128] for g in range(groups)
                ]
                put(block, top, jnp.concatenate(rest, axis=0))
            copies[block].start()
    for copy in copies:
        copy.wait()


def weave(x, y, per, groups, unit, first, stride):
    sources = x.shape[0]
    vmem, anywhere = pl.BlockSpec(memory_space=pltpu.VMEM), pl.BlockSpec(memory_space=pl.ANY)
    operands = [x, jnp.asarray(weaver(unit))] + ([] if y is None else [y])
    return pl.pallas_call(
        functools.partial(weave_kernel, per, groups, unit, first, stride),
        in_specs=[vmem, vmem] + ([] if y is None else [anywhere]),
        out_specs=anywhere,
        out_shape=jax.ShapeDtypeStruct((per, sources * stride), jnp.bfloat16),
        scratch_shapes=[
            pltpu.VMEM((per, sources * unit * sources), jnp.bfloat16),
            pltpu.SemaphoreType.DMA((sources,)),
        ],
        input_output_aliases={} if y is None else {2: 0},
        compiler_params=pltpu.CompilerParams(vmem_limit_bytes=12 * 2**20),
        name="weave",
    )(*operands)


def exchange(x):
    return lax.all_to_all(x, AXIS, split_axis=0, concat_axis=0, tiled=True)


def staged(x, other):
    me = lax.axis_index(AXIS)
    devices = lax.axis_size(AXIS)
    blocks, masks = [x], [0]
    for low, bits in STAGES:
        ways = 2**bits
        mine = lax.bitwise_and(lax.shift_right_logical(me, low), ways - 1)
        width = blocks[0].shape[0] // ways
        groups = []
        for mask in range(ways):
            at = lax.bitwise_xor(mine, mask) * width
            cut = [lax.dynamic_slice_in_dim(block, at, width) for block in blocks]
            cut = cut[0] if len(cut) == 1 else jnp.concatenate(cut, axis=0)
            if mask:
                route = [(i, i ^ (mask << low)) for i in range(devices)]
                if low == STAGES[0][0] and mask == TIE:
                    ahead, other = lax.optimization_barrier((lax.ppermute(cut[:ROWS], AXIS, route), other))
                    cut = jnp.concatenate([ahead, lax.ppermute(cut[ROWS:], AXIS, route)], axis=0)
                else:
                    cut = lax.ppermute(cut, AXIS, route)
            groups.append(cut)
        masks = [(mask << low) ^ old for mask in range(ways) for old in masks]
        blocks = [group[at : at + width] for group in groups for at in range(0, group.shape[0], width)]
    return groups, masks, other


def shards(activations, conv_weight, conv_bias, conv_gain, mlp_gain, w_in, w_out):
    devices = lax.axis_size(AXIS)
    rows, channels = activations.shape
    unit, per = rows // devices, channels // devices
    weights = (conv_weight, conv_bias, conv_gain, mlp_gain, w_in, w_out)
    spare = ROWS - per
    groups = per // spare if 0 < spare < per and per % spare == 0 else 1
    part = unit // CHUNKS
    half = part // 2
    even = half % ROWS == 0 and 128 % part == 0 and devices * part % ((groups + 1) * 128) == 0
    if groups > 1 and even and devices == 2 ** sum(bits for _, bits in STAGES):
        size = rows // CHUNKS
        every = tuple(range(devices))
        towers = []
        for c in range(CHUNKS):
            if c == 0:
                x = activations[:size].reshape(devices, 2, half, channels)
                parts, masks, whole = staged(x[:, 1].reshape(-1, channels), x[:, 0])
                parts = [exchange(whole), *parts]
                layout = [(every, False, 0)]
                held = devices // (len(parts) - 1)
                for i in range(len(parts) - 1):
                    layout.append((tuple(masks[i * held : (i + 1) * held]), True, half))
            else:
                x = lax.optimization_barrier(activations)[c * size : (c + 1) * size]
                parts, layout = [exchange(x)], [(every, False, 0)]
            parts = [x.reshape(-1, channels) for x in parts]
            towers.append(tower(parts, tuple(layout), *weights, part, per, groups))
        y = None
        for c in range(CHUNKS):
            x = exchange(towers[c].reshape(devices, ROWS, -1))
            y = weave(x, y, per, groups, part, c * size, rows)
        return y
    y = tower([exchange(activations)], ((tuple(range(devices)), False, 0),), *weights, unit, per, 1)
    y = exchange(y.reshape(devices, per, rows))
    y = y.reshape(devices, per, devices, unit).transpose(1, 2, 0, 3)
    return y.reshape(per, devices * rows)


def solution(mesh):
    in_specs = (P(AXIS, None), P(), P(), P(), P(), P(), P())
    return jax.shard_map(shards, mesh=mesh, in_specs=in_specs, out_specs=P(AXIS, None), check_vma=False)
```

```python
import functools

import jax
import jax.numpy as jnp
import numpy as np
from jax import lax
from jax.experimental import pallas as pl
from jax.experimental.pallas import tpu as pltpu
from jax.sharding import PartitionSpec as P

AXIS = "seq"
CHUNKS = 2
TIE = 1
STAGES = ((3, 2), (1, 2), (0, 1))
TILE = 256
ROWS = 16


def rms_scale(wide, gain):
    inverse = lax.rsqrt(jnp.mean(wide * wide, axis=-1, keepdims=True) + 1e-06)
    return (wide * inverse * gain).astype(jnp.bfloat16)


def gelu(x):
    return (0.5 * x) * (1.0 + lax.erf(x * np.float32(np.sqrt(0.5))))


def dot(a, b):
    return jnp.dot(a, b, preferred_element_type=jnp.float32)


def tower_kernel(
    tile, unit, groups, layout, me_ref, taps_ref, bias_ref, gain_conv_ref, gain_mlp_ref, in_ref, out_ref, pick_hbm, *refs
):
    *x_refs, y_ref, pick_ref, state_ref, normed_ref, sem = refs
    fetch = pltpu.make_async_copy(pick_hbm, pick_ref, sem)
    layer = pl.program_id(0)
    layers = pl.num_programs(0)
    rows, channels = state_ref.shape
    pad = (normed_ref.shape[1] - rows) // 2
    now = lax.rem(layer, 2)

    @pl.when(layer == 0)
    def _():
        for slot in range(2):
            normed_ref[slot, :pad] = jnp.zeros((pad, channels), jnp.bfloat16)
            normed_ref[slot, pad + rows :] = jnp.zeros((pad, channels), jnp.bfloat16)
        for x_ref, (blocks, relative, offset) in zip(x_refs, layout):
            width = x_ref.shape[0] // len(blocks)
            if width == unit and not relative:
                state_ref[...] = x_ref[...]
                continue
            for i, block in enumerate(blocks):
                block = lax.bitwise_xor(me_ref[0], block) if relative else block
                at = pl.multiple_of(block * unit + offset, ROWS)
                state_ref[pl.ds(at, width)] = x_ref[i * width : (i + 1) * width]
        for start in range(0, rows, tile):
            wide = state_ref[start : start + tile].astype(jnp.float32)
            normed_ref[0, pad + start : pad + start + tile] = rms_scale(wide, gain_conv_ref[0:1])

    @pl.when(layer == layers - 2)
    def _():
        fetch.start()

    shift = lax.shift_left(unit, layer)
    gain_next = gain_conv_ref[pl.ds(jnp.minimum(layer + 1, layers - 1), 1)]

    bias, gain_mlp = bias_ref[pl.ds(layer, 1)], gain_mlp_ref[pl.ds(layer, 1)]
    starts = range(0, rows, tile)

    def mixed(start):
        near = [
            normed_ref[now, pl.ds(pl.multiple_of(pad + start + offset, ROWS), tile)] for offset in (-shift, 0, shift)
        ]
        pre = dot(jnp.concatenate(near, axis=1), taps_ref[0]) + bias
        return (state_ref[start : start + tile].astype(jnp.float32) + gelu(pre)).astype(jnp.bfloat16)

    def widened(middle):
        inner = rms_scale(middle.astype(jnp.float32), gain_mlp)
        return gelu(dot(inner, in_ref[0])).astype(jnp.bfloat16)

    middles = [mixed(start) for start in starts]
    hiddens = [widened(middle) for middle in middles]
    for start, middle, hidden in zip(starts, middles, hiddens):
        new = (middle.astype(jnp.float32) + dot(hidden, out_ref[0])).astype(jnp.bfloat16)
        state_ref[start : start + tile] = new
        normed_ref[1 - now, pad + start : pad + start + tile] = rms_scale(new.astype(jnp.float32), gain_next)

    @pl.when(layer == layers - 1)
    def _():
        fetch.wait()
        width = y_ref.shape[1] // groups
        for g in range(groups):
            part = state_ref[g * width : (g + 1) * width]
            if groups > 1:
                part = jnp.concatenate([part, state_ref[groups * width :]], axis=1)
            y_ref[:, g * width : (g + 1) * width] = lax.dot_general(
                pick_ref[g], part, (((1,), (1,)), ((), ())), preferred_element_type=jnp.float32
            ).astype(jnp.bfloat16)


def picker(channels, per, groups):
    if groups == 1:
        return np.eye(channels, dtype=np.float32)[None].astype(jnp.bfloat16)
    extra = per // groups
    pick = np.zeros((groups, channels // per * ROWS, 2 * channels), np.float32)
    for g in range(groups):
        for owner in range(channels // per):
            for r in range(per):
                pick[g, owner * ROWS + r, owner * per + r] = 1
            for r in range(extra):
                pick[g, owner * ROWS + per + r, channels + owner * per + g * extra + r] = 1
    return pick.astype(jnp.bfloat16)


def tower(parts, layout, conv_weight, conv_bias, conv_gain, mlp_gain, w_in, w_out, unit, per, groups):
    rows, channels = sum(part.shape[0] for part in parts), parts[0].shape[1]
    layers, _, hidden = w_in.shape
    pick = picker(channels, per, groups)
    out_shape = (pick.shape[1], rows // (groups + 1) * groups if groups > 1 else rows)
    pad = unit * 2 ** (layers - 1)
    tile = TILE if rows % TILE == 0 else rows

    anywhere = pl.BlockSpec(memory_space=pl.ANY)

    def whole(shape):
        return pl.BlockSpec(shape, lambda layer: (0,) * len(shape))

    def of_layer(*shape):
        return pl.BlockSpec((1, *shape), lambda layer: (layer, 0, 0))

    return pl.pallas_call(
        functools.partial(tower_kernel, tile, unit, groups, layout),
        grid=(layers,),
        in_specs=[
            pl.BlockSpec(memory_space=pltpu.SMEM),
            of_layer(3 * channels, channels),
            whole(conv_bias.shape),
            whole(conv_gain.shape),
            whole(mlp_gain.shape),
            of_layer(channels, hidden),
            of_layer(hidden, channels),
            anywhere,
            *[whole(part.shape) for part in parts],
        ],
        out_specs=whole(out_shape),
        out_shape=jax.ShapeDtypeStruct(out_shape, jnp.bfloat16),
        scratch_shapes=[
            pltpu.VMEM(pick.shape, jnp.bfloat16),
            pltpu.VMEM((rows, channels), jnp.bfloat16),
            pltpu.VMEM((2, rows + 2 * pad, channels), jnp.bfloat16),
            pltpu.SemaphoreType.DMA,
        ],
        cost_estimate=pl.CostEstimate(
            flops=2 * rows * conv_weight.size + 4 * rows * w_in.size,
            bytes_accessed=2 * (conv_weight.size + 2 * w_in.size + 2 * rows * channels),
            transcendentals=layers * rows * (channels + hidden),
        ),
        compiler_params=pltpu.CompilerParams(vmem_limit_bytes=56 * 2**20),
        name="tower",
    )(
        lax.axis_index(AXIS).reshape(1).astype(jnp.int32),
        conv_weight.reshape(layers, 3 * channels, channels),
        conv_bias,
        conv_gain,
        mlp_gain,
        w_in,
        w_out,
        jnp.asarray(pick),
        *parts,
    )


def weaver(units):
    lanes = 128 // units
    weave_of = np.zeros((lanes, lanes, units, lanes, lanes, units), np.float32)
    for source in range(lanes):
        for block in range(lanes):
            weave_of[source, block, range(units), block, source, range(units)] = 1
    return weave_of.reshape(lanes * 128, lanes * 128).astype(jnp.bfloat16)


def weave_kernel(per, groups, unit, first, stride, x_ref, weave_ref, *refs):
    y_ref, woven_ref, sems = refs[-3:]
    sources, _, width = x_ref.shape
    extra, part = per // groups, width // groups
    span = unit * sources
    lanes = 128 // unit
    tops, tiles, part_tiles = sources // lanes, width // 128, part // 128
    copies = [
        pltpu.make_async_copy(
            woven_ref.at[:, pl.ds(block * span, span)],
            y_ref.at[:, pl.ds(block * stride + first, span)],
            sems.at[block],
        )
        for block in range(sources)
    ]

    def put(block, top, value):
        at = block * span + top * 128
        woven_ref[:, at : at + 128] = value.astype(jnp.bfloat16)

    swapped = []
    for t in range(tiles):
        cut = slice(t * 128, (t + 1) * 128)
        rows = [
            jnp.concatenate([x_ref[top * lanes + source, :, cut] for source in range(lanes)], axis=1)
            for top in range(tops)
        ]
        swapped.append(dot(jnp.concatenate(rows, axis=0), weave_ref[...]))
        for b in range(lanes):
            for top in range(tops):
                low = top * ROWS
                put(t * lanes + b, top, swapped[t][low : low + per, b * 128 : (b + 1) * 128])
            copies[t * lanes + b].start()
    for t in range(part_tiles):
        for b in range(lanes):
            block = (tiles + t) * lanes + b
            for top in range(tops):
                low = top * ROWS + per
                rest = [
                    swapped[g * part_tiles + t][low : low + extra, b * 128 : (b + 1) * 128] for g in range(groups)
                ]
                put(block, top, jnp.concatenate(rest, axis=0))
            copies[block].start()
    for copy in copies:
        copy.wait()


def weave(x, y, per, groups, unit, first, stride):
    sources = x.shape[0]
    vmem, anywhere = pl.BlockSpec(memory_space=pltpu.VMEM), pl.BlockSpec(memory_space=pl.ANY)
    operands = [x, jnp.asarray(weaver(unit))] + ([] if y is None else [y])
    return pl.pallas_call(
        functools.partial(weave_kernel, per, groups, unit, first, stride),
        in_specs=[vmem, vmem] + ([] if y is None else [anywhere]),
        out_specs=anywhere,
        out_shape=jax.ShapeDtypeStruct((per, sources * stride), jnp.bfloat16),
        scratch_shapes=[
            pltpu.VMEM((per, sources * unit * sources), jnp.bfloat16),
            pltpu.SemaphoreType.DMA((sources,)),
        ],
        input_output_aliases={} if y is None else {2: 0},
        compiler_params=pltpu.CompilerParams(vmem_limit_bytes=12 * 2**20),
        name="weave",
    )(*operands)


def exchange(x):
    return lax.all_to_all(x, AXIS, split_axis=0, concat_axis=0, tiled=True)


def staged(x, other):
    me = lax.axis_index(AXIS)
    devices = lax.axis_size(AXIS)
    blocks, masks = [x], [0]
    for low, bits in STAGES:
        ways = 2**bits
        mine = lax.bitwise_and(lax.shift_right_logical(me, low), ways - 1)
        width = blocks[0].shape[0] // ways
        groups = []
        for mask in range(ways):
            at = lax.bitwise_xor(mine, mask) * width
            cut = [lax.dynamic_slice_in_dim(block, at, width) for block in blocks]
            cut = cut[0] if len(cut) == 1 else jnp.concatenate(cut, axis=0)
            if mask:
                route = [(i, i ^ (mask << low)) for i in range(devices)]
                if low == STAGES[0][0] and mask == TIE:
                    ahead, other = lax.optimization_barrier((lax.ppermute(cut[:ROWS], AXIS, route), other))
                    cut = jnp.concatenate([ahead, lax.ppermute(cut[ROWS:], AXIS, route)], axis=0)
                else:
                    cut = lax.ppermute(cut, AXIS, route)
            groups.append(cut)
        masks = [(mask << low) ^ old for mask in range(ways) for old in masks]
        blocks = [group[at : at + width] for group in groups for at in range(0, group.shape[0], width)]
    return groups, masks, other


def shards(activations, conv_weight, conv_bias, conv_gain, mlp_gain, w_in, w_out):
    devices = lax.axis_size(AXIS)
    rows, channels = activations.shape
    unit, per = rows // devices, channels // devices
    weights = (conv_weight, conv_bias, conv_gain, mlp_gain, w_in, w_out)
    spare = ROWS - per
    groups = per // spare if 0 < spare < per and per % spare == 0 else 1
    part = unit // CHUNKS
    half = part // 2
    even = half % ROWS == 0 and 128 % part == 0 and devices * part % ((groups + 1) * 128) == 0
    if groups > 1 and even and devices == 2 ** sum(bits for _, bits in STAGES):
        size = rows // CHUNKS
        every = tuple(range(devices))
        towers = []
        for c in range(CHUNKS):
            if c == 0:
                x = activations[:size].reshape(devices, 2, half, channels)
                parts, masks, whole = staged(x[:, 1].reshape(-1, channels), x[:, 0])
                settled = parts[-1]
                parts = [exchange(whole), *parts]
                layout = [(every, False, 0)]
                held = devices // (len(parts) - 1)
                for i in range(len(parts) - 1):
                    layout.append((tuple(masks[i * held : (i + 1) * held]), True, half))
            else:
                x = lax.optimization_barrier(activations)[c * size : (c + 1) * size]
                x, _ = lax.optimization_barrier((x, settled))
                parts, layout = [exchange(x)], [(every, False, 0)]
            parts = [x.reshape(-1, channels) for x in parts]
            towers.append(tower(parts, tuple(layout), *weights, part, per, groups))
        y = None
        for c in range(CHUNKS):
            x = exchange(towers[c].reshape(devices, ROWS, -1))
            y = weave(x, y, per, groups, part, c * size, rows)
        return y
    y = tower([exchange(activations)], ((tuple(range(devices)), False, 0),), *weights, unit, per, 1)
    y = exchange(y.reshape(devices, per, rows))
    y = y.reshape(devices, per, devices, unit).transpose(1, 2, 0, 3)
    return y.reshape(per, devices * rows)


def solution(mesh):
    in_specs = (P(AXIS, None), P(), P(), P(), P(), P(), P())
    return jax.shard_map(shards, mesh=mesh, in_specs=in_specs, out_specs=P(AXIS, None), check_vma=False)
```
